256 devices in a mesh: fit: 8 (over x, core), pair: 32 (over z, y).
Axes of the slice: x: 4, y: 4, z: 8, core: 2. Of those that a mesh axis runs over, the one named last changes fastest.
Arguments:
- b_ints: bfloat16 [32, 61440, 256], P(None, ('fit', 'pair')), may hold values from -0.375 to 0.375
- dom_blocks: int32 [32, 4], replicated, may hold values from 0 to 624, as said below
- pair_list: int32 [384, 2], P('pair'), may hold values from 0 to 31, as said below
- fock_tab: bfloat16 [625, 4096], replicated, may hold values from -0.875 to 0.875
- vir_energy: float32 [40000], replicated, may hold values from 1 to 3
- occ_energy: float32 [32], replicated, may hold values from -2 to -0.3
- t_amp: bfloat16 [384, 256, 256], P('pair'), may hold values from -3 to 3
Outputs:
- residual: float32 [384, 256, 256], P('pair', 'fit')
- t_new: bfloat16 [384, 256, 256], P('pair', 'fit')
The draws below stay inside these ranges and needn't reach their ends.
Inputs may be any that keep to these rules, and one draw needn't show every extreme that they name: `dom_blocks`: each row names 4 different blocks; some row names block 0 and block 624. `pair_list`: the 12 pairs of owner g (rows g * 12 to (g + 1) * 12 - 1) have both orbitals among (4 g + r) mod 32 for r = 0 to 3; each owner's first pair is (4 g mod 32, (4 g + 3) mod 32).
All inputs are finite; a program needn't handle non-finite values.
Results may differ from the reference program's by a relative error of at most 0.0015.
Values may be sent and summed in bfloat16 or wider, within the bound.
No kernel may reach another device: no remote copies, remote signals or barrier semaphores. Data moves between devices by JAX's collectives and lax.ppermute only.
A program may use at most 384 MiB of HBM per device.

```python
import jax
import jax.numpy as jnp
from jax import lax

NQ = 61440
NV = 40000
DOMV = 256
NOCC = 32
PD = 12
NPAIR = 384
NVB = 625
DB = 4


def draw_dom_blocks(key, part):
    key = jax.random.fold_in(key, 7)
    row_keys = jax.random.split(key, NOCC)
    picked = jax.vmap(lambda row_key: jax.random.permutation(row_key, NVB)[:DB])(row_keys)
    first_key = jax.random.fold_in(key, 11)
    rest = 1 + jax.random.permutation(first_key, NVB - 2)[:DB - 2]
    head = jnp.array([0, NVB - 1], dtype=jnp.int32)
    first_row = jnp.concatenate([head, rest.astype(jnp.int32)])
    return picked.astype(jnp.int32).at[0].set(first_row)


def draw_pair_list(key, part):
    key = jax.random.fold_in(key, 5)
    rows = jnp.arange(NPAIR, dtype=jnp.int32)
    owners = rows // PD
    offsets = jax.random.randint(key, (NPAIR, 2), 0, 4).astype(jnp.int32)
    leading = (rows % PD == 0)[:, None]
    fixed_pair = jnp.array([[0, 3]], dtype=jnp.int32)
    offsets = jnp.where(leading, fixed_pair, offsets)
    return ((4 * owners[:, None] + offsets) % NOCC).astype(jnp.int32)


def block_levels(own_key, extent, cuts, least, top_value):
    loudness, own = 1.0, jax.random.fold_in(own_key, 6)
    for axis_at, shards_of in cuts:
        draws = jnp.exp(jax.random.uniform(jax.random.fold_in(own, axis_at), (shards_of,), jnp.float32, least / len(cuts), top_value / len(cuts)))
        loudness = loudness * jnp.repeat(draws, extent[axis_at] // shards_of).reshape([-1 if axis == axis_at else 1 for axis in range(len(extent))])
    return loudness


def bell_draw(own_key, shape, deviation, reach, cuts=(), held_as=jnp.bfloat16):
    values = deviation * jax.random.normal(own_key, shape, jnp.float32)
    if cuts:
        values = values * block_levels(own_key, shape, cuts, -0.22, 0.18)
    return jnp.clip(values, -reach, reach).astype(held_as)


def setup_inputs(seed: int = 0) -> dict:
    keys = jax.random.split(jax.random.key(seed), 8)
    return {
        "b_ints": bell_draw(keys[0], (NOCC, NQ, DOMV), (NQ ** 0.5) ** -0.5, 0.375, ((1, 256),)),
        "dom_blocks": draw_dom_blocks(jax.random.fold_in(keys[7], 71), 0),
        "pair_list": draw_pair_list(jax.random.fold_in(keys[7], 71), 0),
        "fock_tab": bell_draw(keys[3], (NVB, 4096), 0.06, 0.875),
        "vir_energy": jnp.clip(jax.random.uniform(keys[4], (NV,), jnp.float32, 1.0, 3.0), 1.0, 3.0),
        "occ_energy": jnp.clip(jax.random.uniform(keys[5], (NOCC,), jnp.float32, -2.0, -0.3), -2.0, -0.3),
        "t_amp": bell_draw(keys[6], (NPAIR, DOMV, DOMV), 0.2, 3.0, ((0, 32),)),
    }


def domain_fock(orbit, dom_blocks, fock_tab, vir_energy):
    blocks = dom_blocks[orbit]
    block_count = blocks.shape[0]
    fock_tiles = jnp.take(fock_tab, blocks, axis=0).reshape(block_count, 64, 64).astype(jnp.float32)
    diag_unit = jnp.eye(block_count, dtype=jnp.float32)
    fock_full = (fock_tiles[:, :, None, :] * diag_unit[:, None, :, None]).reshape(block_count * 64, block_count * 64)
    virt_ids = (blocks[:, None] * 64 + jnp.arange(64, dtype=jnp.int32)[None, :]).reshape(-1)
    energy = jnp.take(vir_energy, virt_ids)
    fock_full = fock_full + jnp.diag(energy)
    return fock_full, jnp.diagonal(fock_full)


def reference(b_ints, dom_blocks, pair_list, fock_tab, vir_energy, occ_energy, t_amp):
    def per_pair(entry_pair):
        orbits, amps = entry_pair
        orb_a = orbits[0]
        orb_b = orbits[1]
        kblock = jnp.dot(b_ints[orb_a].T, b_ints[orb_b], preferred_element_type=jnp.float32)
        fock_a, diag_a = domain_fock(orb_a, dom_blocks, fock_tab, vir_energy)
        fock_b, diag_b = domain_fock(orb_b, dom_blocks, fock_tab, vir_energy)
        amplitude = amps.astype(jnp.float32)
        pair_shift = occ_energy[orb_a] + occ_energy[orb_b]
        resid = kblock + jnp.dot(fock_a, amplitude, precision=lax.Precision.HIGHEST)
        resid = resid + jnp.dot(amplitude, fock_b, precision=lax.Precision.HIGHEST) - pair_shift * amplitude
        denominator = diag_a[:, None] + diag_b[None, :] - pair_shift
        updated = (amplitude - resid / denominator).astype(jnp.bfloat16)
        return resid, updated

    residual, t_new = lax.map(per_pair, (pair_list, t_amp))
    return (residual, t_new)
```

```python
import functools

import jax
import jax.numpy as jnp
from jax import lax
from jax.experimental import pallas as pl
from jax.experimental.pallas import tpu as pltpu
from jax.sharding import Mesh, PartitionSpec as P

FIT = ("x", "core")
PAIR = ("zq", "zp", "y")
OWN = ("zp", "y")
SCALE = 4.0
ORBITALS = 4
HALF = jnp.float16


HALVES = (
    ((0, 0), (0, 1), (1, 0), (1, 1), (0, 2), (2, 0), (0, 3), (3, 0)),
    ((1, 2), (2, 1), (1, 3), (3, 1), (2, 2), (2, 3), (3, 2), (3, 3)),
)


def up(zq):
    return zq ^ 1


def down(zq):
    return ((zq + 1) ^ 1) - 1


def swapped(value, partner):
    return lax.ppermute(value, "zq", [(i, partner(i) % 4) for i in range(4)])


def gram_kernel(blocks, place, ints, *refs):
    keeps, send, full = refs[:4], refs[4], refs[5]
    x, core = place[0], place[1]

    def rows_of(orbital):
        return ints[:, orbital].reshape(-1, ints.shape[-1])

    def emit(at):
        for dx in range(4):
            start = pl.multiple_of(64 * lax.rem(x + dx, 4), 64)
            keeps[dx][at] = full[pl.ds(start + 32 * core, 32), :]
            send[dx, at] = full[pl.ds(start + 32 * (1 - core), 32), :]

    for i in range(ORBITALS):
        wanted = [j for j in range(i, ORBITALS) if (i, j) in blocks]
        if not wanted:
            continue
        left = rows_of(i).T
        for j in wanted:
            product = jnp.dot(left, rows_of(j), preferred_element_type=jnp.float32) * SCALE
            full[...] = product
            emit(blocks.index((i, j)))
            if i != j:
                full[...] = product.T
                emit(blocks.index((j, i)))


def gram(place, ints, blocks):
    nb, width = len(blocks), ints.shape[-1]
    piece = (nb, 32, width)
    whole = pl.BlockSpec(memory_space=pltpu.VMEM)
    *keep, send = pl.pallas_call(
        functools.partial(gram_kernel, blocks),
        out_shape=[jax.ShapeDtypeStruct(piece, jnp.float32)] * 4
        + [jax.ShapeDtypeStruct((4, *piece), jnp.float32)],
        in_specs=[pl.BlockSpec(memory_space=pltpu.SMEM), whole],
        out_specs=[whole] * 5,
        scratch_shapes=[pltpu.VMEM((width, width), jnp.float32)],
        compiler_params=pltpu.CompilerParams(vmem_limit_bytes=40 << 20),
        cost_estimate=pl.CostEstimate(
            flops=2 * nb * width * width * ints.shape[0] * ints.shape[2],
            bytes_accessed=nb * width * width * 8,
            transcendentals=0,
        ),
    )(place, ints)
    return keep, send


def fock_kernel(slots, place, occ, fock, energy, amp, w_ref, den_ref, row_ref):
    p = pl.program_id(0)
    block = place[3]
    off = pl.multiple_of(32 * place[1], 32)
    sa, sb = slots[2 * p], slots[2 * p + 1]
    shift = occ[sa] + occ[sb]
    rows = amp[0, pl.ds(off, 32), :]
    rows32 = rows.astype(jnp.float32)
    fa = fock[4 * sa + block, pl.ds(off, 32), :]
    ea = energy[4 * sa + block]
    left = jnp.dot(fa, amp[0], preferred_element_type=jnp.float32)
    on_diag = lax.broadcasted_iota(jnp.int32, (32, 64), 1) == (
        lax.broadcasted_iota(jnp.int32, (32, 64), 0) + off
    )
    ea_col = jnp.sum(jnp.where(on_diag, ea, 0.0), axis=1, keepdims=True)
    fa_col = jnp.sum(jnp.where(on_diag, fa.astype(jnp.float32), 0.0), axis=1, keepdims=True)
    unit = lax.broadcasted_iota(jnp.int32, (64, 64), 0) == lax.broadcasted_iota(
        jnp.int32, (64, 64), 1
    )
    right, eb, db = [], [], []
    for k in range(4):
        fb = fock[4 * sb + k]
        right.append(
            jnp.dot(rows[:, 64 * k : 64 * k + 64], fb, preferred_element_type=jnp.float32)
        )
        eb.append(energy[4 * sb + k])
        fb_diag = jnp.sum(jnp.where(unit, fb.astype(jnp.float32), 0.0), axis=0, keepdims=True)
        db.append(fb_diag + eb[-1])
    right = jnp.concatenate(right, axis=1) + rows32 * jnp.concatenate(eb, axis=1)
    left = left + ea_col * rows32
    w_ref[0] = left + right - shift * rows32
    den_ref[0] = (fa_col + ea_col) + jnp.concatenate(db, axis=1) - shift
    row_ref[0] = rows32


def fock_terms(slots, place, occ, fock, energy, t_amp):
    pairs = t_amp.shape[0]
    out = jax.ShapeDtypeStruct((pairs, 32, 256), jnp.float32)
    row_spec = pl.BlockSpec((1, 32, 256), lambda p, *_: (p, 0, 0))
    return pl.pallas_call(
        fock_kernel,
        out_shape=(out, out, out),
        grid_spec=pltpu.PrefetchScalarGridSpec(
            num_scalar_prefetch=3,
            grid=(pairs,),
            in_specs=[
                pl.BlockSpec((16, 64, 64), lambda p, *_: (0, 0, 0)),
                pl.BlockSpec((16, 1, 64), lambda p, *_: (0, 0, 0)),
                pl.BlockSpec((1, 64, 256), lambda p, slots, place, occ: (p, place[3], 0)),
            ],
            out_specs=(row_spec, row_spec, row_spec),
        ),
        cost_estimate=pl.CostEstimate(
            flops=pairs * 32 * 64 * 256 * 4, bytes_accessed=pairs * 32 * 256 * 16, transcendentals=0
        ),
    )(slots, place, occ, fock, energy, t_amp)


def final_kernel(pairs, index, a_ref, b_ref, w_ref, den_ref, row_ref, res_ref, new_ref, full):
    size = a_ref.shape[0]
    full[:size] = a_ref[...]
    full[size:] = b_ref[...]
    for p in range(pairs):
        res = full[index[p]] * (1.0 / SCALE) + w_ref[p]
        res_ref[p] = res
        new_ref[p] = (row_ref[p] - res / den_ref[p]).astype(jnp.bfloat16)


def finish(index, sums, w, den, rows):
    pairs = w.shape[0]
    whole = pl.BlockSpec(memory_space=pltpu.VMEM)
    smem = pl.BlockSpec(memory_space=pltpu.SMEM)
    return pl.pallas_call(
        functools.partial(final_kernel, pairs),
        out_shape=(
            jax.ShapeDtypeStruct(w.shape, jnp.float32),
            jax.ShapeDtypeStruct(w.shape, jnp.bfloat16),
        ),
        in_specs=[smem] + [whole] * 5,
        out_specs=(whole, whole),
        scratch_shapes=[pltpu.VMEM((ORBITALS * ORBITALS, *w.shape[1:]), jnp.float32)],
    )(index, *sums, w, den, rows)


def shifted(value, axis, by):
    count = lax.axis_size(axis)
    return lax.ppermute(value, axis, [(i, (i + by) % count) for i in range(count)])


def to_float(value):
    return value.astype(jnp.float32)


def over_cores(keep, send):
    other = shifted(send.astype(HALF), "core", 1)
    both = [keep[d] + to_float(other[d]) for d in range(4)]
    return both[0], [both[d].astype(HALF) for d in (2, 1, 3)]


def over_x(pieces):
    return [shifted(piece, "x", d) for piece, d in zip(pieces, (2, 1, 3))]


def local(b_ints, dom_blocks, pair_list, fock_tab, vir_energy, occ_energy, t_amp):
    barrier = lax.optimization_barrier
    x, core, group = lax.axis_index("x"), lax.axis_index("core"), lax.axis_index(OWN)
    place = jnp.stack([x, core, x, x]).astype(jnp.int32)
    first = ORBITALS * group
    ints = b_ints.reshape(8, ORBITALS, *b_ints.shape[1:])
    ints = lax.all_to_all(ints, OWN, 0, 0)

    ids = lax.dynamic_slice_in_dim(dom_blocks, first, ORBITALS, 0).reshape(16)
    fock = jnp.take(fock_tab, ids, axis=0, mode="clip").reshape(16, 64, 64)
    energy = jnp.take(vir_energy.reshape(-1, 64), ids, axis=0, mode="clip").reshape(16, 1, 64)
    occ = lax.dynamic_slice_in_dim(occ_energy, first, ORBITALS, 0)
    slots = ((pair_list - first) % 32).astype(jnp.int32)
    order = [block for half in HALVES for block in half]
    index_of = [order.index((i, j)) for i in range(ORBITALS) for j in range(ORBITALS)]
    index = jnp.take(
        jnp.array(index_of, jnp.int32), slots[:, 0] * ORBITALS + slots[:, 1], mode="clip"
    )
    w, den, rows = fock_terms(slots.reshape(-1), place, occ, fock, energy, t_amp)
    ints, index, w, den, rows = barrier((ints, index, w, den, rows))

    own, pieces = over_cores(*gram(place, ints, HALVES[0]))
    parts = over_x(pieces)
    own_b, pieces_b = over_cores(*gram(place, ints, HALVES[1]))
    parts_b = over_x(pieces_b)
    total = own + sum(to_float(part) for part in parts)
    near = swapped(total.astype(HALF), up)
    total = total + to_float(near)
    total_b = own_b + sum(to_float(part) for part in parts_b)
    total = total + to_float(swapped(total.astype(HALF), down))
    total_b = total_b + to_float(swapped(total_b.astype(HALF), down))
    total_b = total_b + to_float(swapped(total_b.astype(HALF), up))
    return finish(index, [total, total_b], w, den, rows)


def solution(mesh):
    fine = Mesh(mesh.devices.reshape(4, 2, 4, 2, 4), FIT + PAIR)
    placed = (
        P(None, FIT + PAIR, None),
        P(),
        P(PAIR, None),
        P(),
        P(),
        P(),
        P(PAIR, None, None),
    )
    return jax.shard_map(
        local,
        mesh=fine,
        in_specs=placed,
        out_specs=(P(PAIR, FIT, None), P(PAIR, FIT, None)),
        check_vma=False,
    )
```
